32 devices in a mesh: rep: 2 (over y), head: 16 (over z, x, core).
Axes of the slice: x: 2, y: 2, z: 4, core: 2. Of those that a mesh axis runs over, the one named last changes fastest.
Arguments:
- query: bfloat16 [2, 2048, 8192], P('rep', 'head'), may hold values from -16 to 16
- key: bfloat16 [2, 2048, 1024], P('rep', 'head'), may hold values from -16 to 16
- value: bfloat16 [2, 2048, 1024], P('rep', 'head'), may hold values from -6 to 6
- lengths: int32 [2, 8], P('rep'), may hold values from 1 to 1024, 2048 in all within a row
Outputs:
- attended: bfloat16 [2, 2048, 8192], P('rep', 'head')
The draws below stay inside these ranges and needn't reach their ends.
Inputs may be any that keep to these rules, and one draw needn't show every extreme that they name: Each slab's 8 lengths sum to 2048, and the longest is exactly 1024.
All inputs are finite; a program needn't handle non-finite values.
Results may differ from the reference program's by a relative error of at most 0.0038.
Values may be sent and summed in bfloat16 or wider, within the bound.
No kernel may reach another device: no remote copies, remote signals or barrier semaphores. Data moves between devices by JAX's collectives and lax.ppermute only.
A program may use at most 64 MiB of HBM per device.

```python
import math
import jax
import jax.numpy as jnp
import numpy as np
from jax import lax

Q_HEADS = 64
KV_HEADS = 8
HEAD_DIM = 128
DOCS = 8
REPLICAS = 2
SLAB = 2048
MAXDOC = 1024


def shared_rows(key):
    return jax.random.normal(jax.random.fold_in(key, 11), (REPLICAS, SLAB, KV_HEADS * HEAD_DIM), jnp.float32)


def draw_key(key, part):
    base = shared_rows(key)
    return jnp.clip(base, -6.0, 6.0).astype(jnp.bfloat16)


def draw_query(key, part):
    key = jax.random.fold_in(key, 5)
    fresh = jax.random.normal(key, (REPLICAS, SLAB, Q_HEADS * HEAD_DIM), jnp.float32)
    return jnp.clip(fresh, -6.0, 6.0).astype(jnp.bfloat16)


def levels(key, shape, split, smallest, high):
    level, own = 1.0, jax.random.fold_in(key, 6)
    for dim, parts in split:
        steps = jnp.exp(jax.random.uniform(jax.random.fold_in(own, dim), (parts,), jnp.float32, smallest / len(split), high / len(split)))
        level = level * jnp.repeat(steps, shape[dim] // parts).reshape([-1 if axis == dim else 1 for axis in range(len(shape))])
    return level


def split_up(amount, total, most, slope):
    weights = [(1 << 20) // math.isqrt(standing ** slope) + 1 for standing in range(2, amount + 1)]
    rest, holding = total - most - (amount - 1), [1] * (amount - 1)
    while rest > 0:
        candidates = [i for i in range(amount - 1) if holding[i] < most]
        pool, left = sum([weights[i] for i in candidates]), rest
        for i in candidates:
            more = min(most - holding[i], max(1, left * weights[i] // pool), rest)
            holding[i] = holding[i] + more
            rest = rest - more
    return np.array([most] + holding)


def ragged(key, amount, total, reach, skew):
    if amount == 2:
        one = jax.random.randint(key, (), max(1, total - reach), min(reach, total - 1) + 1)
        return jnp.stack([one, total - one])
    sizes = jnp.asarray(split_up(amount, total, reach, skew), jnp.int32)
    couples = (amount - 1) // 2
    source_of, receiver = sizes[1:1 + 2 * couples:2], sizes[2:2 + 2 * couples:2]
    room = jnp.minimum(source_of - 1, reach - receiver)
    passed = jax.random.randint(jax.random.fold_in(key, 1), (couples,), 0, 1 << 20) % (room + 1)
    sizes = sizes.at[1:1 + 2 * couples:2].set(source_of - passed).at[2:2 + 2 * couples:2].set(receiver + passed)
    return sizes[jax.random.permutation(jax.random.fold_in(key, 2), amount)]


def centred(stream_key, dims, deviation, most, pieces=(), kind=jnp.bfloat16):
    values = deviation * jax.random.normal(stream_key, dims, jnp.float32)
    if pieces:
        values = values * levels(stream_key, dims, pieces, -0.22, 0.18)
    return jnp.clip(values, -most, most).astype(kind)


def setup_inputs(seed: int = 0) -> dict:
    seeds = jax.random.split(jax.random.key(seed), 5)
    return {
        "query": draw_query(jax.random.fold_in(seeds[4], 71), 0),
        "key": draw_key(jax.random.fold_in(seeds[4], 71), 0),
        "value": centred(seeds[2], (REPLICAS, SLAB, KV_HEADS * HEAD_DIM), 1.0, 6.0, ((0, 2), (1, 16))),
        "lengths": jax.vmap(lambda own: ragged(own, DOCS, SLAB, MAXDOC, 2))(jax.random.split(seeds[3], REPLICAS)).reshape((REPLICAS, DOCS)).astype(jnp.int32),
    }


def doc_starts(doc_lengths, count):
    ends = jnp.cumsum(doc_lengths)
    places = jnp.arange(count, dtype=jnp.int32)
    picked = jnp.where(ends[None, :] <= places[:, None], doc_lengths[None, :], 0)
    return jnp.sum(picked, axis=1).astype(jnp.int32)


def attend_tile(queries, keys, values, starts, index, tile):
    heads = queries.shape[1]
    q_block = lax.dynamic_slice_in_dim(queries, index * tile, tile, 0).astype(jnp.float32)
    q_pos = index * tile + jnp.arange(tile, dtype=jnp.int32)
    q_start = lax.dynamic_slice_in_dim(starts, index * tile, tile, 0)
    first = (q_start[0] // tile).astype(jnp.int32)
    scale = float(HEAD_DIM) ** -0.5

    def visit(block, carry):
        top, total, accum = carry
        k_block = lax.dynamic_slice_in_dim(keys, block * tile, tile, 0).astype(jnp.float32)
        v_block = lax.dynamic_slice_in_dim(values, block * tile, tile, 0).astype(jnp.float32)
        scores = jnp.einsum("qhd,khd->hqk", q_block, k_block) * scale
        k_pos = block * tile + jnp.arange(tile, dtype=jnp.int32)
        allowed = (k_pos[None, :] <= q_pos[:, None]) & (k_pos[None, :] >= q_start[:, None])
        scores = jnp.where(allowed[None], scores, jnp.float32(-1e30))
        new_top = jnp.maximum(top, jnp.max(scores, axis=2))
        weights = jnp.where(allowed[None], jnp.exp(scores - new_top[:, :, None]), jnp.float32(0.0))
        factor = jnp.exp(top - new_top)
        rounded = weights.astype(jnp.bfloat16).astype(jnp.float32)
        accum = accum * factor[:, :, None] + jnp.einsum("hqk,khd->hqd", rounded, v_block)
        total = total * factor + jnp.sum(weights, axis=2)
        return new_top, total, accum

    start_state = (jnp.full((heads, tile), -1e30, jnp.float32), jnp.zeros((heads, tile), jnp.float32),
                   jnp.zeros((heads, tile, HEAD_DIM), jnp.float32))
    top, total, accum = lax.fori_loop(first, (index + 1).astype(jnp.int32), visit, start_state)
    result = (accum / total[:, :, None]).astype(jnp.bfloat16)
    return jnp.transpose(result, (1, 0, 2))


def one_slab(inputs):
    queries, keys, values, doc_lengths = inputs
    count = queries.shape[0]
    tile = min(512, count)
    starts = doc_starts(doc_lengths, count)
    queries = queries.reshape(count, Q_HEADS, HEAD_DIM)
    group = Q_HEADS // KV_HEADS
    keys = jnp.repeat(keys.reshape(count, KV_HEADS, HEAD_DIM), group, axis=1)
    values = jnp.repeat(values.reshape(count, KV_HEADS, HEAD_DIM), group, axis=1)

    def per_tile(index):
        return attend_tile(queries, keys, values, starts, index, tile)

    blocks = lax.map(per_tile, jnp.arange(count // tile, dtype=jnp.int32))
    return blocks.reshape(count, Q_HEADS * HEAD_DIM)


def reference(query, key, value, lengths):
    return lax.map(one_slab, (query, key, value, lengths))
```

```python
import functools
import math

import jax
import jax.numpy as jnp
from jax import lax
from jax.experimental import pallas as pl
from jax.experimental.pallas import tpu as pltpu
from jax.sharding import PartitionSpec as P

Q_HEADS = 64
KV_HEADS = 8
HEAD_DIM = 128
GROUP = Q_HEADS // KV_HEADS
BIG = -1e30
FAR = 1 << 29
SCALE = float(HEAD_DIM) ** -0.5 * math.log2(math.e)
ROWS = 256
LOWEST, HIGHEST = 2.0 ** -40, 2.0 ** 100


def fill(slots, kv_refs, ka, va, core, tok):
    d = HEAD_DIM
    for at, arrays in slots:
        def copy(ref, at=at):
            ka[at * tok:(at + 1) * tok, :d] = ref[0]
            va[at * tok:(at + 1) * tok, :d] = ref[1]
        if len(arrays) == 1:
            copy(kv_refs[arrays[0]])
        else:
            for pick, array in enumerate(arrays):
                pl.when(core == pick)(functools.partial(copy, kv_refs[array]))


def prepare(info, total, docs, qa, ka, va, tok):
    d = HEAD_DIM
    q_pos = info[total] + lax.broadcasted_iota(jnp.int32, (tok, tok), 1)
    start = jnp.zeros((tok, tok), jnp.int32)
    end = jnp.int32(0)
    for doc in range(docs):
        length = info[total + 3 + doc]
        end = end + length
        start = start + jnp.where(q_pos >= end, length, 0)
    row = lax.broadcasted_iota(jnp.int32, (tok, tok), 0)
    for b in range(total):
        k_pos = info[b] + row
        allowed = (k_pos <= q_pos) & (k_pos >= start)
        ka[b * tok:(b + 1) * tok, d:] = jnp.where(allowed, 0.0, BIG).astype(jnp.bfloat16)
    one = (row == lax.broadcasted_iota(jnp.int32, (tok, tok), 1)).astype(jnp.float32)
    for j in range(GROUP):
        qa[j * tok:(j + 1) * tok, d:] = one.astype(jnp.bfloat16)
    va[:, d:] = jnp.ones((total * tok, d), jnp.bfloat16)


def scores(qa, ka, first, rows, low, high):
    return lax.dot_general(qa[first:first + rows, :], ka[low:high, :], (((1,), (1,)), ((), ())),
                           preferred_element_type=jnp.float32)


def sums(qa, ka, va, low, high, tok, take):
    ahead = scores(qa, ka, 0, ROWS, low, high)
    for first in range(0, GROUP * tok, ROWS):
        s = ahead
        if first + ROWS < GROUP * tok:
            ahead = scores(qa, ka, first + ROWS, ROWS, low, high)
        p = jnp.exp2(s * SCALE).astype(jnp.bfloat16)
        o = jnp.dot(p, va[low:high, :], preferred_element_type=jnp.float32)
        for j in range(ROWS // tok):
            take(first // tok + j, o[j * tok:(j + 1) * tok, :HEAD_DIM], o[j * tok:(j + 1) * tok, HEAD_DIM:])


def by_column(info, total, slots, cut, run):
    if cut is None:
        run(slots)
    else:
        column, count = cut
        pl.when(info[total + 1] == column)(lambda: run(slots[:count]))
        pl.when(info[total + 1] != column)(lambda: run(slots))


def early_kernel(total, slots, cut, docs, tok, info, q_ref, *rest):
    kv_refs, (acc_ref, sum_ref, qa, ka, va) = rest[:-5], rest[-5:]
    d = HEAD_DIM
    pl.when(pl.program_id(0) == 0)(lambda: prepare(info, total, docs, qa, ka, va, tok))
    for j in range(GROUP):
        qa[j * tok:(j + 1) * tok, :d] = q_ref[:, j * d:(j + 1) * d]

    def run(part):
        fill(part, kv_refs, ka, va, info[total + 2], tok)
        lane = lax.broadcasted_iota(jnp.int32, (tok, d), 1)
        packed = [jnp.zeros((tok, d), jnp.float32)]

        def take(j, acc, row_sum):
            acc_ref[:, j * d:(j + 1) * d] = acc
            packed[0] = jnp.where(lane == j, row_sum, packed[0])

        sums(qa, ka, va, part[0][0] * tok, (part[-1][0] + 1) * tok, tok, take)
        sum_ref[...] = packed[0]

    by_column(info, total, slots, cut, run)


def late_kernel(total, early, slots, cut, docs, tok, info, q_ref, acc_ref, sum_ref, *rest):
    kv_refs, (o_ref, qa, ka, va, bad) = rest[:-5], rest[-5:]
    d = HEAD_DIM
    pl.when(pl.program_id(0) == 0)(lambda: prepare(info, total, docs, qa, ka, va, tok))
    for j in range(GROUP):
        qa[j * tok:(j + 1) * tok, :d] = q_ref[:, j * d:(j + 1) * d]
    core = info[total + 2]

    def run(part):
        fill(part, kv_refs, ka, va, core, tok)
        off = [jnp.zeros((tok, d), jnp.float32)]

        def take(j, acc, row_sum):
            row_sum = row_sum + sum_ref[:, j:j + 1]
            fine = (row_sum >= LOWEST) & (row_sum <= HIGHEST)
            off[0] = jnp.where(fine, off[0], 1.0)
            o_ref[:, j * d:(j + 1) * d] = ((acc + acc_ref[:, j * d:(j + 1) * d]) / row_sum).astype(jnp.bfloat16)

        sums(qa, ka, va, part[0][0] * tok, (part[-1][0] + 1) * tok, tok, take)
        bad[...] = jnp.max(off[0], axis=0, keepdims=True)

    by_column(info, total, slots, cut, run)

    @pl.when(jnp.max(bad[...]) > 0.0)
    def _():
        fill(early + slots, kv_refs, ka, va, core, tok)
        for j in range(GROUP):
            s = scores(qa, ka, j * tok, tok, 0, total * tok)
            top = jnp.max(s, axis=1, keepdims=True)
            p = jnp.exp2((s - top) * SCALE).astype(jnp.bfloat16)
            o = jnp.dot(p, va[...], preferred_element_type=jnp.float32)
            o_ref[:, j * d:(j + 1) * d] = (o[:, :d] / o[:, d:]).astype(jnp.bfloat16)


def attend(body, q, state, arrays, info, total, keys, outs, scratch):
    tok = q.shape[0]
    d = HEAD_DIM
    wide = pl.BlockSpec((tok, GROUP * d), lambda g, info: (0, g))
    thin = pl.BlockSpec((None, tok, d), lambda g, info: (g, 0, 0))
    narrow = pl.BlockSpec((2, tok, d), lambda g, info: (0, 0, g))
    grid_spec = pltpu.PrefetchScalarGridSpec(
        num_scalar_prefetch=1,
        grid=(KV_HEADS,),
        in_specs=[wide] + [wide, thin][:len(state)] + [narrow] * len(arrays),
        out_specs=[wide, thin][:len(outs)],
        scratch_shapes=[
            pltpu.VMEM((GROUP * tok, 2 * d), jnp.bfloat16),
            pltpu.VMEM((total * tok, 2 * d), jnp.bfloat16),
            pltpu.VMEM((total * tok, 2 * d), jnp.bfloat16),
        ] + scratch,
    )
    return pl.pallas_call(
        body,
        out_shape=outs,
        grid_spec=grid_spec,
        compiler_params=pltpu.CompilerParams(vmem_limit_bytes=(24 if total <= 16 else 44) * 1024 * 1024),
        cost_estimate=pl.CostEstimate(flops=8 * Q_HEADS * tok * keys * d,
                                      bytes_accessed=4 * q.size + 4 * keys * KV_HEADS * d,
                                      transcendentals=Q_HEADS * tok * keys),
    )(info, q, *state, *arrays)


class Route:
    def __init__(self, devices):
        self.plane = math.isqrt(devices)
        self.cols = self.plane // 2
        self.levels = devices // self.plane
        self.reach = devices // 2 // self.plane

    def at(self, z, x, c):
        return z * self.plane + x * 2 + c

    def everyone(self, level, cores=(0, 1)):
        return [(z, x, c) for z in range(level, self.levels) for x in range(self.cols) for c in cores]

    def wanted(self, level, src, dst):
        return src < dst if level == 0 else src > dst if level == self.reach else True

    def up(self, level):
        return [(self.at(z - 1, x, c), self.at(z, x, c)) for z, x, c in self.everyone(level)]

    def across(self, level, dx, cores=(0, 1)):
        return [(self.at(z, (x - dx) % self.cols, c), self.at(z, x, c)) for z, x, c in self.everyone(level, cores)
                if self.wanted(level, (x - dx) % self.cols, x)]

    def climb(self, dx, cores):
        return [(self.at(z - 1, x, c), self.at(z, x, c)) for z, x, c in self.everyone(self.reach, cores)
                if self.wanted(self.reach, (x - dx) % self.cols, x)]

    def over(self, level, dx, cores=(0, 1)):
        return [(self.at(z, x, 1 - c), self.at(z, x, c)) for z, x, c in self.everyone(level, cores)
                if (self.wanted(level, 1 - c, c) if dx == 0 else self.wanted(level, (x - dx) % self.cols, x))]

    def carry(self, block, attend_early):
        send = lambda array, pairs: lax.ppermute(array, "head", pairs)
        reach, columns = self.reach, range(1, self.cols)
        got = {(0, 0, 0): [block]}

        def swap(level, dx):
            got[level, dx, 1] = [send(got[level, dx, 0][0], self.over(level, dx))]

        state = None
        for level in range(reach):
            held = got[level, 0, 0][0]
            new = [send(held, self.up(level + 1))]
            new += [send(held, self.across(level, dx)) for dx in columns]
            if level:
                for dx in columns:
                    swap(level - 1, dx)
                swap(level, 0)
                if level == 1:
                    state = attend_early(got)
                    new, state = lax.optimization_barrier((new, state))
            else:
                swap(0, 0)
            if level != 1:
                new = lax.optimization_barrier(new)
            got[level + 1, 0, 0] = [new[0]]
            for dx in columns:
                got[level, dx, 0] = [new[dx]]
        for dx in columns:
            got[reach, dx, 0] = [send(got[reach, 0, 0][0], self.across(reach, dx, (0,))),
                                 send(got[reach - 1, dx, 0][0], self.climb(dx, (1,)))]
        swap(reach, 0)
        for dx in columns:
            swap(reach - 1, dx)
            got[reach, dx, 1] = [send(got[reach, dx, 0][1 - c], self.over(reach, dx, (c,))) for c in range(2)]
        return got, state

    def order(self):
        names = [(level, dx, other) for dx in range(self.cols) for level in range(self.reach + 1) for other in range(2)]
        early = [n for n in names if n[0] == 0 or (n[0] == 1 and n[1] == 0 and self.reach > 1)]
        late = [n for n in names if n not in early]
        partial = lambda n: n[1] > 0 and n[0] in (0, self.reach)
        return sorted(early, key=partial), sorted(late, key=partial)

    def block(self, name, me):
        level, dx, other = name
        z, x, c = me // self.plane, me % self.plane // 2, me % 2
        col = (x - dx + self.cols) % self.cols
        core = 1 - c if other else c
        want = self.wanted(level, core, c) if dx == 0 else self.wanted(level, col, x)
        held = (z >= level) & (want | (dx == 0 and other == 0))
        return jnp.where(held, self.at(z - level, col, core), -1)


def local(query, key, value, lengths):
    tok = query.shape[1]
    docs = lengths.shape[1]
    d = HEAD_DIM
    me = lax.axis_index("head")
    route = Route(lax.axis_size("head"))
    early, late = route.order()
    total = len(early) + len(late)
    base = [jnp.where(b >= 0, b * tok, FAR) for b in (route.block(name, me) for name in early + late)]
    info = jnp.stack(base + [me * tok, me % route.plane // 2, me % 2])
    info = jnp.concatenate([info, lengths[0]]).astype(jnp.int32)

    q = query[0]
    cut = (lambda column, part: (column, len(part) - 2)) if route.cols == 2 else (lambda column, part: None)

    def listed(got, names, at):
        arrays, slots = [], []
        for name in names:
            slots.append((at + len(slots), list(range(len(arrays), len(arrays) + len(got[name])))))
            arrays += got[name]
        return arrays, slots

    def attend_early(got):
        arrays, slots = listed(got, early, 0)
        return attend(
            functools.partial(early_kernel, total, slots, cut(0, slots), docs, tok), q, [], arrays, info, total,
            len(slots) * tok,
            [jax.ShapeDtypeStruct(q.shape, jnp.float32), jax.ShapeDtypeStruct((KV_HEADS, tok, d), jnp.float32)], [])

    got, state = route.carry(jnp.stack([key[0], value[0]]), attend_early)
    arrays, slots = listed(got, early + late, 0)
    first, last = slots[:len(early)], slots[len(early):]
    out, = attend(
        functools.partial(late_kernel, total, first, last, cut(1, last), docs, tok), q, state, arrays, info, total,
        len(last) * tok, [jax.ShapeDtypeStruct(q.shape, jnp.bfloat16)], [pltpu.VMEM((1, d), jnp.float32)])
    return out[None]


def solution(mesh):
    placed = (
        P("rep", "head", None),
        P("rep", "head", None),
        P("rep", "head", None),
        P("rep", None),
    )
    return jax.shard_map(
        local, mesh=mesh, in_specs=placed, out_specs=P("rep", "head", None), check_vma=False
    )
```

```python
import functools
import math

import jax
import jax.numpy as jnp
from jax import lax
from jax.experimental import pallas as pl
from jax.experimental.pallas import tpu as pltpu
from jax.sharding import PartitionSpec as P

Q_HEADS = 64
KV_HEADS = 8
HEAD_DIM = 128
GROUP = Q_HEADS // KV_HEADS
BIG = -1e30
FAR = 1 << 29
SCALE = float(HEAD_DIM) ** -0.5 * math.log2(math.e)
UNIT = 2
TILE = 256
LOWEST, HIGHEST = 2.0 ** -40, 2.0 ** 100
COST = 16


def masks(slots, info, total, docs, tok):
    q_pos = info[total] + lax.broadcasted_iota(jnp.int32, (tok, tok), 1)
    start = jnp.zeros((tok, tok), jnp.int32)
    end = jnp.int32(0)
    for doc in range(docs):
        length = info[total + 2 + doc]
        end = end + length
        start = start + jnp.where(q_pos >= end, length, 0)
    row = lax.broadcasted_iota(jnp.int32, (tok, tok), 0)
    for at, _ in slots:
        k_pos = info[at] + row
        yield jnp.where((k_pos <= q_pos) & (k_pos >= start), 0.0, BIG).astype(jnp.bfloat16)


def scores(q, k):
    return lax.dot_general(q, k, (((1,), (1,)), ((), ())), preferred_element_type=jnp.float32)


def kernel(form, info, *refs):
    total, early, late, cut, docs, tok, rows, count, is_late = form
    d = HEAD_DIM
    wide = GROUP * d
    refs = list(refs)
    q_ref = refs.pop(0)
    state = [refs.pop(0), refs.pop(0)] if is_late else []
    kv_refs, refs = refs[:count], refs[count:]
    slots = late if is_late else early
    if is_late:
        out_ref, mask_ref, out_buf, limits, everything, sems = refs
    else:
        acc_ref, sum_ref, mask_ref = refs
    row = lax.broadcasted_iota(jnp.int32, (tok, tok), 0)
    eye = (row == lax.broadcasted_iota(jnp.int32, (tok, tok), 1)).astype(jnp.float32).astype(jnp.bfloat16)
    one = jnp.ones((tok, d), jnp.bfloat16)

    def span(g, width):
        return pl.ds(pl.multiple_of(g * width, width), width)

    def queries(g, first, rows):
        return jnp.concatenate([jnp.concatenate([q_ref[:, span(g * GROUP + j, d)], eye], axis=1)
                                for j in range(first // tok, (first + rows) // tok)], axis=0)

    def result(u, buf, h):
        return pltpu.make_async_copy(out_buf.at[buf, h], out_ref.at[:, span(u * UNIT + h, wide)], sems.at[buf, h])

    def attend(part, u, buf):
        keys = len(part) * tok
        lane = lax.broadcasted_iota(jnp.int32, (tok, d), 1)
        packed = [jnp.zeros((tok, d), jnp.float32) for _ in range(UNIT)]
        least = most = jnp.ones((tok, d), jnp.float32)
        pieces = [(h, first) for h in range(UNIT) for first in range(0, GROUP * tok, rows)]
        step = TILE // tok
        tiles = [range(low, min(low + step, len(part))) for low in range(0, len(part), step)]

        def score(piece, tile):
            g = u * UNIT + piece[0]
            k = [jnp.concatenate([kv_refs[part[n][1]][0, :, span(g, d)], mask_ref[n * tok:(n + 1) * tok, :]], axis=1)
                 for n in tile]
            return scores(queries(g, piece[1], rows), jnp.concatenate(k, axis=0))

        ahead = [score(pieces[0], tile) for tile in tiles]
        for i, (h, first) in enumerate(pieces):
            g = u * UNIT + h
            s, ahead, p = ahead, [], []
            for n, tile in enumerate(tiles):
                p.append(jnp.exp2(s[n] * SCALE).astype(jnp.bfloat16))
                if i + 1 < len(pieces):
                    ahead.append(score(pieces[i + 1], tile))
            v = [jnp.concatenate([kv_refs[array][1, :, span(g, d)], one], axis=1) for _, array in part]
            o = jnp.dot(jnp.concatenate(p, axis=1), jnp.concatenate(v, axis=0), preferred_element_type=jnp.float32)
            for n in range(rows // tok):
                j = first // tok + n
                acc, row_sum = o[n * tok:(n + 1) * tok, :d], o[n * tok:(n + 1) * tok, d:]
                if is_late:
                    row_sum = row_sum + state[1][g, :, j:j + 1]
                    least, most = jnp.minimum(least, row_sum), jnp.maximum(most, row_sum)
                    share = pl.reciprocal(row_sum, approx=True)
                    share = share * (2.0 - row_sum * share)
                    acc = (acc + state[0][:, span(g * GROUP + j, d)]) * share
                    out_buf[buf, h, :, j * d:(j + 1) * d] = acc.astype(jnp.bfloat16)
                else:
                    packed[h] = jnp.where(lane == j, row_sum, packed[h])
                    acc_ref[:, span(g * GROUP + j, d)] = acc
        if is_late:
            limits[0] = jnp.minimum(limits[0], least)
            limits[1] = jnp.maximum(limits[1], most)
        else:
            for h in range(UNIT):
                sum_ref[u * UNIT + h] = packed[h]

    def run(part):
        units = KV_HEADS // UNIT
        for n, mask in enumerate(masks(part, info, total, docs, tok)):
            mask_ref[n * tok:(n + 1) * tok, :] = mask
        if is_late:
            limits[...] = jnp.ones((2, tok, d), jnp.float32)

        def step(u, carry):
            buf = lax.rem(u, 2)
            if is_late:
                @pl.when(u > 1)
                def _():
                    for h in range(UNIT):
                        result(u - 2, buf, h).wait()
            attend(part, u, buf)
            if is_late:
                for h in range(UNIT):
                    result(u, buf, h).start()
            return carry

        lax.fori_loop(0, units, step, 0)
        if is_late:
            for u in range(units - 2, units):
                for h in range(UNIT):
                    result(u, u % 2, h).wait()

    if cut is None:
        run(slots)
    else:
        for column, picked in enumerate(cut):
            pl.when(info[total + 1] == column)(functools.partial(run, [slots[n] for n in picked]))

    if is_late:
        inside = (limits[0] >= LOWEST) & (limits[1] <= HIGHEST)

        @pl.when(jnp.max(jnp.where(inside, 0.0, 1.0)) > 0.0)
        def _():
            for n, mask in enumerate(masks(early + late, info, total, docs, tok)):
                everything[0, n * tok:(n + 1) * tok, d:] = mask
                everything[1, n * tok:(n + 1) * tok, d:] = one

            def again(g, carry):
                for n, (_, array) in enumerate(early + late):
                    copy = pltpu.make_async_copy(kv_refs[array].at[:, :, span(g, d)],
                                                 everything.at[:, n * tok:(n + 1) * tok, :d], sems.at[0, 0])
                    copy.start()
                    copy.wait()
                for j in range(GROUP):
                    s = scores(queries(g, j * tok, tok), everything[0])
                    top = jnp.max(s, axis=1, keepdims=True)
                    p = jnp.exp2((s - top) * SCALE).astype(jnp.bfloat16)
                    o = jnp.dot(p, everything[1], preferred_element_type=jnp.float32)
                    out_buf[0, 0, :, j * d:(j + 1) * d] = (o[:, :d] / o[:, d:]).astype(jnp.bfloat16)
                store = pltpu.make_async_copy(out_buf.at[0, 0], out_ref.at[:, span(g, wide)], sems.at[0, 0])
                store.start()
                store.wait()
                return carry

            lax.fori_loop(0, KV_HEADS, again, 0)


def attend(form, q, state, arrays, info, outs):
    total, early, late, cut, docs, tok, rows, count, is_late = form
    d = HEAD_DIM
    n = max(len(picked) for picked in cut) if cut else len(late if is_late else early)
    anywhere, here = pl.BlockSpec(memory_space=pl.ANY), pl.BlockSpec(memory_space=pltpu.VMEM)
    scratch = [pltpu.VMEM((n * tok, d), jnp.bfloat16)]
    if is_late:
        scratch += [
            pltpu.VMEM((2, UNIT, tok, GROUP * d), jnp.bfloat16),
            pltpu.VMEM((2, tok, d), jnp.float32),
            pltpu.VMEM((2, total * tok, 2 * d), jnp.bfloat16),
            pltpu.SemaphoreType.DMA((2, UNIT)),
        ]
    mine = {array for _, array in (late if is_late else early)}
    return pl.pallas_call(
        functools.partial(kernel, form),
        out_shape=outs,
        in_specs=[pl.BlockSpec(memory_space=pltpu.SMEM)] + [here] * (1 + len(state))
        + [here if i in mine else anywhere for i in range(len(arrays))],
        out_specs=[anywhere if is_late else here] * len(outs),
        scratch_shapes=scratch,
        compiler_params=pltpu.CompilerParams(vmem_limit_bytes=(28 if total <= 16 else 60) * 1024 * 1024),
        cost_estimate=pl.CostEstimate(flops=COST * q.size, bytes_accessed=q.size, transcendentals=0),
    )(info, q, *state, *arrays)


def join(key, value):
    first = lax.broadcasted_iota(jnp.int32, (2, 1, 1), 0) == 0
    return jnp.where(first, key, value)


class Route:
    def __init__(self, devices):
        self.plane = math.isqrt(devices)
        self.cols = self.plane // 2
        self.levels = devices // self.plane
        self.reach = devices // 2 // self.plane

    def at(self, z, x, c):
        return z * self.plane + x * 2 + c

    def everyone(self, level, cores=(0, 1)):
        return [(z, x, c) for z in range(level, self.levels) for x in range(self.cols) for c in cores]

    def wanted(self, level, src, dst):
        return src < dst if level == 0 else src > dst if level == self.reach else True

    def up(self, level):
        return [(self.at(z - 1, x, c), self.at(z, x, c)) for z, x, c in self.everyone(level)]

    def across(self, level, dx, cores=(0, 1)):
        return [(self.at(z, (x - dx) % self.cols, c), self.at(z, x, c)) for z, x, c in self.everyone(level, cores)
                if self.wanted(level, (x - dx) % self.cols, x)]

    def climb(self, dx, cores):
        return [(self.at(z - 1, x, c), self.at(z, x, c)) for z, x, c in self.everyone(self.reach, cores)
                if self.wanted(self.reach, (x - dx) % self.cols, x)]

    def over(self, level, dx, cores=(0, 1)):
        return [(self.at(z, x, 1 - c), self.at(z, x, c)) for z, x, c in self.everyone(level, cores)
                if (self.wanted(level, 1 - c, c) if dx == 0 else self.wanted(level, (x - dx) % self.cols, x))]

    def carry(self, block, core, attend_early):
        send = lambda array, pairs: lax.ppermute(array, "head", pairs)
        reach, columns = self.reach, range(1, self.cols)
        got = {(0, 0, 0): block}

        def swap(level, dx):
            got[level, dx, 1] = send(got[level, dx, 0], self.over(level, dx))

        def tie(names, *more):
            arrays, more = lax.optimization_barrier(([got[name] for name in names], more))
            got.update(zip(names, arrays))
            return more

        state = None
        for level in range(reach):
            got[level + 1, 0, 0] = send(got[level, 0, 0], self.up(level + 1))
            for dx in columns:
                got[level, dx, 0] = send(got[level, 0, 0], self.across(level, dx))
            if level == 0:
                swap(0, 0)
            if level == 1:
                swap(1, 0)
                tie([(0, dx, 0) for dx in columns] + [(0, 0, 1)])
                state = attend_early(got)
                state, = tie([(0, dx, 0) for dx in columns] + [(1, dx, 0) for dx in columns] + [(2, 0, 0)], state)
            elif level:
                tie([(level, dx, 0) for dx in columns] + [(level + 1, 0, 0)])
        for dx in columns:
            pairs = self.across(reach, dx, (0,)) + self.climb(dx, (1,))
            got[reach, dx, 0] = send(jnp.where(core == 0, got[reach, 0, 0], got[reach - 1, dx, 0]), pairs)
        for level in range(2, reach + 1):
            swap(level, 0)
        for dx in columns:
            for level in range(reach + 1):
                swap(level, dx)
        return got, state

    def order(self):
        names = [(level, dx, other) for dx in range(self.cols) for level in range(self.reach + 1) for other in range(2)]
        early = [n for n in names if n[1] == 0 and n[0] < 2]
        late = [n for n in names if n not in early]
        partial = lambda n: n[1] > 0 and n[0] in (0, self.reach)
        return sorted(early, key=partial), sorted(late, key=partial)

    def block(self, name, me):
        level, dx, other = name
        z, x, c = me // self.plane, me % self.plane // 2, me % 2
        col = (x - dx + self.cols) % self.cols
        core = 1 - c if other else c
        want = self.wanted(level, core, c) if dx == 0 else self.wanted(level, col, x)
        held = (z >= level) & (want | (dx == 0 and other == 0))
        return jnp.where(held, self.at(z - level, col, core), -1)


def local(query, key, value, lengths):
    tok = query.shape[1]
    docs = lengths.shape[1]
    d = HEAD_DIM
    me = lax.axis_index("head")
    route = Route(lax.axis_size("head"))
    early, late = route.order()
    total = len(early) + len(late)
    base = [jnp.where(b >= 0, b * tok, FAR) for b in (route.block(name, me) for name in early + late)]
    info = jnp.stack(base + [me * tok, me % route.plane // 2])
    info = jnp.concatenate([info, lengths[0]]).astype(jnp.int32)

    q = query[0]
    def forms(part):
        if route.cols != 2:
            return None
        lacking = (0, route.reach)
        return [[n for n, name in enumerate(part) if name[1] == 0 or name[0] != lacking[x]] for x in range(2)]

    def listed(got, names, at):
        return [got[name] for name in names], [(at + n, n) for n in range(len(names))]

    def attend_early(got):
        arrays, slots = listed(got, early, 0)
        return attend((total, slots, [], forms(early), docs, tok, rows, len(arrays), False), q, [], arrays, info,
                      [jax.ShapeDtypeStruct(q.shape, jnp.float32),
                       jax.ShapeDtypeStruct((KV_HEADS, tok, d), jnp.float32)])

    rows = 512 if total <= 16 else 128
    got, state = route.carry(join(key, value), me % 2, attend_early)
    arrays, slots = listed(got, early + late, 0)
    first, last = slots[:len(early)], slots[len(early):]
    out, = attend((total, first, last, forms(late), docs, tok, rows, len(arrays), True), q, state, arrays, info,
                  [jax.ShapeDtypeStruct(q.shape, jnp.bfloat16)])
    return out[None]


def solution(mesh):
    placed = (
        P("rep", "head", None),
        P("rep", "head", None),
        P("rep", "head", None),
        P("rep", None),
    )
    return jax.shard_map(
        local, mesh=mesh, in_specs=placed, out_specs=P("rep", "head", None), check_vma=False
    )
```

```python
import functools
import math

import jax
import jax.numpy as jnp
from jax import lax
from jax.experimental import pallas as pl
from jax.experimental.pallas import tpu as pltpu
from jax.sharding import PartitionSpec as P

Q_HEADS = 64
KV_HEADS = 8
HEAD_DIM = 128
GROUP = Q_HEADS // KV_HEADS
BIG = -1e30
FAR = 1 << 29
SCALE = float(HEAD_DIM) ** -0.5 * math.log2(math.e)
UNIT = 2
TILE = 256
LOWEST, HIGHEST = 2.0 ** -40, 2.0 ** 100
COST = 16


def masks(slots, info, total, docs, tok):
    q_pos = info[total] + lax.broadcasted_iota(jnp.int32, (tok, tok), 1)
    start = jnp.zeros((tok, tok), jnp.int32)
    end = jnp.int32(0)
    for doc in range(docs):
        length = info[total + 2 + doc]
        end = end + length
        start = start + jnp.where(q_pos >= end, length, 0)
    row = lax.broadcasted_iota(jnp.int32, (tok, tok), 0)
    for at, _ in slots:
        k_pos = info[at] + row
        yield jnp.where((k_pos <= q_pos) & (k_pos >= start), 0.0, BIG).astype(jnp.bfloat16)


def scores(q, k):
    return lax.dot_general(q, k, (((1,), (1,)), ((), ())), preferred_element_type=jnp.float32)


def kernel(form, info, *refs):
    total, before, slots, cut, docs, tok, rows, count, has_state, is_last = form
    d = HEAD_DIM
    wide = GROUP * d
    refs = list(refs)
    q_ref = refs.pop(0)
    state = [refs.pop(0), refs.pop(0)] if has_state else []
    kv_refs, refs = refs[:count], refs[count:]
    if is_last:
        out_ref, mask_ref, out_buf, limits, everything, sems = refs
    else:
        acc_ref, sum_ref, mask_ref = refs
    row = lax.broadcasted_iota(jnp.int32, (tok, tok), 0)
    eye = (row == lax.broadcasted_iota(jnp.int32, (tok, tok), 1)).astype(jnp.float32).astype(jnp.bfloat16)
    one = jnp.ones((tok, d), jnp.bfloat16)

    def span(g, width):
        return pl.ds(pl.multiple_of(g * width, width), width)

    def queries(g, first, rows):
        return jnp.concatenate([jnp.concatenate([q_ref[:, span(g * GROUP + j, d)], eye], axis=1)
                                for j in range(first // tok, (first + rows) // tok)], axis=0)

    def result(u, buf, h):
        return pltpu.make_async_copy(out_buf.at[buf, h], out_ref.at[:, span(u * UNIT + h, wide)], sems.at[buf, h])

    def attend(part, u, buf):
        keys = len(part) * tok
        lane = lax.broadcasted_iota(jnp.int32, (tok, d), 1)
        packed = [jnp.zeros((tok, d), jnp.float32) for _ in range(UNIT)]
        least = most = jnp.ones((tok, d), jnp.float32)
        pieces = [(h, first) for h in range(UNIT) for first in range(0, GROUP * tok, rows)]
        step = TILE // tok
        tiles = [range(low, min(low + step, len(part))) for low in range(0, len(part), step)]

        def score(piece, tile):
            g = u * UNIT + piece[0]
            k = [jnp.concatenate([kv_refs[part[n][1]][0, :, span(g, d)], mask_ref[n * tok:(n + 1) * tok, :]], axis=1)
                 for n in tile]
            return scores(queries(g, piece[1], rows), jnp.concatenate(k, axis=0))

        ahead = [score(pieces[0], tile) for tile in tiles]
        for i, (h, first) in enumerate(pieces):
            g = u * UNIT + h
            s, ahead, p = ahead, [], []
            for n, tile in enumerate(tiles):
                p.append(jnp.exp2(s[n] * SCALE).astype(jnp.bfloat16))
                if i + 1 < len(pieces):
                    ahead.append(score(pieces[i + 1], tile))
            v = [jnp.concatenate([kv_refs[array][1, :, span(g, d)], one], axis=1) for _, array in part]
            o = jnp.dot(jnp.concatenate(p, axis=1), jnp.concatenate(v, axis=0), preferred_element_type=jnp.float32)
            for n in range(rows // tok):
                j = first // tok + n
                acc, row_sum = o[n * tok:(n + 1) * tok, :d], o[n * tok:(n + 1) * tok, d:]
                if has_state:
                    acc = acc + state[0][:, span(g * GROUP + j, d)]
                if is_last:
                    row_sum = row_sum + state[1][g, :, j:j + 1]
                    least, most = jnp.minimum(least, row_sum), jnp.maximum(most, row_sum)
                    share = pl.reciprocal(row_sum, approx=True)
                    share = share * (2.0 - row_sum * share)
                    out_buf[buf, h, :, j * d:(j + 1) * d] = (acc * share).astype(jnp.bfloat16)
                else:
                    packed[h] = jnp.where(lane == j, row_sum, packed[h])
                    acc_ref[:, span(g * GROUP + j, d)] = acc
        if is_last:
            limits[0] = jnp.minimum(limits[0], least)
            limits[1] = jnp.maximum(limits[1], most)
        else:
            for h in range(UNIT):
                sum_ref[u * UNIT + h] = packed[h] + state[1][u * UNIT + h] if has_state else packed[h]

    def run(part):
        units = KV_HEADS // UNIT
        for n, mask in enumerate(masks(part, info, total, docs, tok)):
            mask_ref[n * tok:(n + 1) * tok, :] = mask
        if is_last:
            limits[...] = jnp.ones((2, tok, d), jnp.float32)

        def step(u, carry):
            buf = lax.rem(u, 2)
            if is_last:
                @pl.when(u > 1)
                def _():
                    for h in range(UNIT):
                        result(u - 2, buf, h).wait()
            attend(part, u, buf)
            if is_last:
                for h in range(UNIT):
                    result(u, buf, h).start()
            return carry

        lax.fori_loop(0, units, step, 0)
        if is_last:
            for u in range(units - 2, units):
                for h in range(UNIT):
                    result(u, u % 2, h).wait()

    if cut is None:
        run(slots)
    else:
        for column, picked in enumerate(cut):
            pl.when(info[total + 1] == column)(functools.partial(run, [slots[n] for n in picked]))

    if is_last:
        inside = (limits[0] >= LOWEST) & (limits[1] <= HIGHEST)

        @pl.when(jnp.max(jnp.where(inside, 0.0, 1.0)) > 0.0)
        def _():
            for n, mask in enumerate(masks(before + slots, info, total, docs, tok)):
                everything[0, n * tok:(n + 1) * tok, d:] = mask
                everything[1, n * tok:(n + 1) * tok, d:] = one

            def again(g, carry):
                for n, (_, array) in enumerate(before + slots):
                    copy = pltpu.make_async_copy(kv_refs[array].at[:, :, span(g, d)],
                                                 everything.at[:, n * tok:(n + 1) * tok, :d], sems.at[0, 0])
                    copy.start()
                    copy.wait()
                for j in range(GROUP):
                    s = scores(queries(g, j * tok, tok), everything[0])
                    top = jnp.max(s, axis=1, keepdims=True)
                    p = jnp.exp2((s - top) * SCALE).astype(jnp.bfloat16)
                    o = jnp.dot(p, everything[1], preferred_element_type=jnp.float32)
                    out_buf[0, 0, :, j * d:(j + 1) * d] = (o[:, :d] / o[:, d:]).astype(jnp.bfloat16)
                store = pltpu.make_async_copy(out_buf.at[0, 0], out_ref.at[:, span(g, wide)], sems.at[0, 0])
                store.start()
                store.wait()
                return carry

            lax.fori_loop(0, KV_HEADS, again, 0)


def attend(form, q, state, arrays, info, outs):
    total, before, slots, cut, docs, tok, rows, count, has_state, is_last = form
    d = HEAD_DIM
    n = max(len(picked) for picked in cut) if cut else len(slots)
    anywhere, here = pl.BlockSpec(memory_space=pl.ANY), pl.BlockSpec(memory_space=pltpu.VMEM)
    scratch = [pltpu.VMEM((n * tok, d), jnp.bfloat16)]
    if is_last:
        scratch += [
            pltpu.VMEM((2, UNIT, tok, GROUP * d), jnp.bfloat16),
            pltpu.VMEM((2, tok, d), jnp.float32),
            pltpu.VMEM((2, total * tok, 2 * d), jnp.bfloat16),
            pltpu.SemaphoreType.DMA((2, UNIT)),
        ]
    mine = {array for _, array in slots}
    return pl.pallas_call(
        functools.partial(kernel, form),
        out_shape=outs,
        in_specs=[pl.BlockSpec(memory_space=pltpu.SMEM)] + [here] * (1 + len(state))
        + [here if i in mine else anywhere for i in range(len(arrays))],
        out_specs=[anywhere if is_last else here] * len(outs),
        scratch_shapes=scratch,
        compiler_params=pltpu.CompilerParams(vmem_limit_bytes=(16 if total <= 16 else 60) * 1024 * 1024),
        cost_estimate=pl.CostEstimate(flops=COST * q.size, bytes_accessed=q.size, transcendentals=0),
    )(info, q, *state, *arrays)


def join(key, value):
    first = lax.broadcasted_iota(jnp.int32, (2, 1, 1), 0) == 0
    return jnp.where(first, key, value)


class Route:
    def __init__(self, devices):
        self.plane = math.isqrt(devices)
        self.cols = self.plane // 2
        self.levels = devices // self.plane
        self.reach = devices // 2 // self.plane

    def at(self, z, x, c):
        return z * self.plane + x * 2 + c

    def everyone(self, level, cores=(0, 1)):
        return [(z, x, c) for z in range(level, self.levels) for x in range(self.cols) for c in cores]

    def wanted(self, level, src, dst):
        return src < dst if level == 0 else src > dst if level == self.reach else True

    def up(self, level):
        return [(self.at(z - 1, x, c), self.at(z, x, c)) for z, x, c in self.everyone(level)]

    def across(self, level, dx, cores=(0, 1)):
        return [(self.at(z, (x - dx) % self.cols, c), self.at(z, x, c)) for z, x, c in self.everyone(level, cores)
                if self.wanted(level, (x - dx) % self.cols, x)]

    def climb(self, dx, cores):
        return [(self.at(z - 1, x, c), self.at(z, x, c)) for z, x, c in self.everyone(self.reach, cores)
                if self.wanted(self.reach, (x - dx) % self.cols, x)]

    def over(self, level, dx, cores=(0, 1)):
        return [(self.at(z, x, 1 - c), self.at(z, x, c)) for z, x, c in self.everyone(level, cores)
                if (self.wanted(level, 1 - c, c) if dx == 0 else self.wanted(level, (x - dx) % self.cols, x))]

    def carry(self, block, core, attend_early, attend_middle):
        send = lambda array, pairs: lax.ppermute(array, "head", pairs)
        reach, columns = self.reach, range(1, self.cols)
        got = {(0, 0, 0): block}

        def swap(level, dx):
            got[level, dx, 1] = send(got[level, dx, 0], self.over(level, dx))

        def tie(names, *more):
            arrays, more = lax.optimization_barrier(([got[name] for name in names], more))
            got.update(zip(names, arrays))
            return more

        state = None
        for level in range(reach):
            got[level + 1, 0, 0] = send(got[level, 0, 0], self.up(level + 1))
            for dx in columns:
                got[level, dx, 0] = send(got[level, 0, 0], self.across(level, dx))
            if level == 0:
                swap(0, 0)
            if level == 1:
                swap(1, 0)
                tie([(0, dx, 0) for dx in columns] + [(0, 0, 1)])
                state = attend_early(got)
                state, = tie([(0, dx, 0) for dx in columns] + [(1, dx, 0) for dx in columns] + [(2, 0, 0)], state)
            elif level:
                tie([(level, dx, 0) for dx in columns] + [(level + 1, 0, 0)])
        for dx in columns:
            pairs = self.across(reach, dx, (0,)) + self.climb(dx, (1,))
            got[reach, dx, 0] = send(jnp.where(core == 0, got[reach, 0, 0], got[reach - 1, dx, 0]), pairs)
        for level in range(2, reach + 1):
            swap(level, 0)
        for dx in columns:
            for level in range(reach):
                swap(level, dx)
        state, = tie([(reach, dx, 0) for dx in columns], attend_middle(got, state))
        for dx in columns:
            swap(reach, dx)
        return got, state

    def order(self):
        names = [(level, dx, other) for dx in range(self.cols) for level in range(self.reach + 1) for other in range(2)]
        early = [n for n in names if n[1] == 0 and n[0] < 2]
        middle = [n for n in names if n[2] == 0 and (n[0] > 1 if n[1] == 0 else 0 < n[0] < self.reach)]
        return early, middle, [n for n in names if n not in early + middle]

    def block(self, name, me):
        level, dx, other = name
        z, x, c = me // self.plane, me % self.plane // 2, me % 2
        col = (x - dx + self.cols) % self.cols
        core = 1 - c if other else c
        want = self.wanted(level, core, c) if dx == 0 else self.wanted(level, col, x)
        held = (z >= level) & (want | (dx == 0 and other == 0))
        return jnp.where(held, self.at(z - level, col, core), -1)


def local(query, key, value, lengths):
    tok = query.shape[1]
    docs = lengths.shape[1]
    d = HEAD_DIM
    me = lax.axis_index("head")
    route = Route(lax.axis_size("head"))
    parts = route.order()
    names = sum(parts, [])
    total = len(names)
    base = [jnp.where(b >= 0, b * tok, FAR) for b in (route.block(name, me) for name in names)]
    info = jnp.stack(base + [me * tok, me % route.plane // 2])
    info = jnp.concatenate([info, lengths[0]]).astype(jnp.int32)
    q = query[0]
    rows = 512 if total <= 16 else 128

    def forms(part):
        if route.cols != 2 or all(name[1] == 0 or 0 < name[0] < route.reach for name in part):
            return None
        lacking = (0, route.reach)
        return [[n for n, name in enumerate(part) if name[1] == 0 or name[0] != lacking[x]] for x in range(2)]

    def work(got, stage, state):
        first = sum(len(part) for part in parts[:stage])
        is_last = stage + 1 == len(parts)
        known = names if is_last else parts[stage]
        slots = [(first + n, n + (first if is_last else 0)) for n in range(len(parts[stage]))]
        before = [(n, n) for n in range(first)]
        outs = [jax.ShapeDtypeStruct(q.shape, jnp.float32), jax.ShapeDtypeStruct((KV_HEADS, tok, d), jnp.float32)]
        if is_last:
            outs = [jax.ShapeDtypeStruct(q.shape, jnp.bfloat16)]
        form = (total, before, slots, forms(parts[stage]), docs, tok, rows, len(known), bool(state), is_last)
        return attend(form, q, state, [got[name] for name in known], info, outs)

    got, state = route.carry(join(key, value), me % 2, lambda got: work(got, 0, []), lambda got, state: work(got, 1, state))
    out, = work(got, 2, state)
    return out[None]


def solution(mesh):
    placed = (
        P("rep", "head", None),
        P("rep", "head", None),
        P("rep", "head", None),
        P("rep", None),
    )
    return jax.shard_map(
        local, mesh=mesh, in_specs=placed, out_specs=P("rep", "head", None), check_vma=False
    )
```

```python
import functools
import math

import jax
import jax.numpy as jnp
from jax import lax
from jax.experimental import pallas as pl
from jax.experimental.pallas import tpu as pltpu
from jax.sharding import PartitionSpec as P

Q_HEADS = 64
KV_HEADS = 8
HEAD_DIM = 128
GROUP = Q_HEADS // KV_HEADS
BIG = -1e30
FAR = 1 << 29
SCALE = float(HEAD_DIM) ** -0.5 * math.log2(math.e)
UNIT = 4
TILE = 256
LOWEST, HIGHEST = 2.0 ** -40, 2.0 ** 100
COST = 16


def masks(slots, info, total, docs, tok):
    q_pos = info[total] + lax.broadcasted_iota(jnp.int32, (tok, tok), 1)
    start = jnp.zeros((tok, tok), jnp.int32)
    end = jnp.int32(0)
    for doc in range(docs):
        length = info[total + 2 + doc]
        end = end + length
        start = start + jnp.where(q_pos >= end, length, 0)
    row = lax.broadcasted_iota(jnp.int32, (tok, tok), 0)
    for at, _ in slots:
        k_pos = info[at] + row
        yield jnp.where((k_pos <= q_pos) & (k_pos >= start), 0.0, BIG).astype(jnp.bfloat16)


def scores(q, k):
    return lax.dot_general(q, k, (((1,), (1,)), ((), ())), preferred_element_type=jnp.float32)


def kernel(form, info, *refs):
    total, before, slots, cut, docs, tok, rows, count, has_state, is_last = form
    d = HEAD_DIM
    wide = GROUP * d
    refs = list(refs)
    q_ref = refs.pop(0)
    state = [refs.pop(0), refs.pop(0)] if has_state else []
    kv_refs, refs = refs[:count], refs[count:]
    if is_last:
        out_ref, mask_ref, out_buf, limits, everything, sems = refs
    else:
        acc_ref, sum_ref, mask_ref = refs
    row = lax.broadcasted_iota(jnp.int32, (tok, tok), 0)
    eye = (row == lax.broadcasted_iota(jnp.int32, (tok, tok), 1)).astype(jnp.float32).astype(jnp.bfloat16)
    one = jnp.ones((tok, d), jnp.bfloat16)

    def span(g, width):
        return pl.ds(pl.multiple_of(g * width, width), width)

    def queries(g, first, rows):
        return jnp.concatenate([jnp.concatenate([q_ref[:, span(g * GROUP + j, d)], eye], axis=1)
                                for j in range(first // tok, (first + rows) // tok)], axis=0)

    def result(u, buf, h):
        return pltpu.make_async_copy(out_buf.at[buf, h], out_ref.at[:, span(u * UNIT + h, wide)], sems.at[buf, h])

    def attend(part, u, buf):
        keys = len(part) * tok
        lane = lax.broadcasted_iota(jnp.int32, (tok, d), 1)
        packed = [jnp.zeros((tok, d), jnp.float32) for _ in range(UNIT)]
        least = most = jnp.ones((tok, d), jnp.float32)
        pieces = [(h, first) for h in range(UNIT) for first in range(0, GROUP * tok, rows)]
        step = TILE // tok
        tiles = [range(low, min(low + step, len(part))) for low in range(0, len(part), step)]

        def score(piece, tile):
            g = u * UNIT + piece[0]
            k = [jnp.concatenate([kv_refs[part[n][1]][0, :, span(g, d)], mask_ref[n * tok:(n + 1) * tok, :]], axis=1)
                 for n in tile]
            return scores(queries(g, piece[1], rows), jnp.concatenate(k, axis=0))

        ahead = [score(pieces[0], tile) for tile in tiles]
        for i, (h, first) in enumerate(pieces):
            g = u * UNIT + h
            s, ahead, p = ahead, [], []
            for n, tile in enumerate(tiles):
                p.append(jnp.exp2(s[n] * SCALE).astype(jnp.bfloat16))
                if i + 1 < len(pieces):
                    ahead.append(score(pieces[i + 1], tile))
            v = [jnp.concatenate([kv_refs[array][1, :, span(g, d)], one], axis=1) for _, array in part]
            o = jnp.dot(jnp.concatenate(p, axis=1), jnp.concatenate(v, axis=0), preferred_element_type=jnp.float32)
            for n in range(rows // tok):
                j = first // tok + n
                acc, row_sum = o[n * tok:(n + 1) * tok, :d], o[n * tok:(n + 1) * tok, d:]
                if has_state:
                    acc = acc + state[0][:, span(g * GROUP + j, d)]
                if is_last:
                    row_sum = row_sum + state[1][g, :, j:j + 1]
                    least, most = jnp.minimum(least, row_sum), jnp.maximum(most, row_sum)
                    share = pl.reciprocal(row_sum, approx=True)
                    share = share * (2.0 - row_sum * share)
                    out_buf[buf, h, :, j * d:(j + 1) * d] = (acc * share).astype(jnp.bfloat16)
                else:
                    packed[h] = jnp.where(lane == j, row_sum, packed[h])
                    acc_ref[:, span(g * GROUP + j, d)] = acc
            if is_last and first + rows == GROUP * tok:
                result(u, buf, h).start()
        if is_last:
            limits[0] = jnp.minimum(limits[0], least)
            limits[1] = jnp.maximum(limits[1], most)
        else:
            for h in range(UNIT):
                sum_ref[u * UNIT + h] = packed[h] + state[1][u * UNIT + h] if has_state else packed[h]

    def run(part):
        units = KV_HEADS // UNIT
        for n, mask in enumerate(masks(part, info, total, docs, tok)):
            mask_ref[n * tok:(n + 1) * tok, :] = mask
        if is_last:
            limits[...] = jnp.ones((2, tok, d), jnp.float32)

        def step(u, carry):
            buf = lax.rem(u, 2)
            if is_last:
                @pl.when(u > 1)
                def _():
                    for h in range(UNIT):
                        result(u - 2, buf, h).wait()
            attend(part, u, buf)
            return carry

        lax.fori_loop(0, units, step, 0)
        if is_last:
            for u in range(units - 2, units):
                for h in range(UNIT):
                    result(u, u % 2, h).wait()

    if cut is None:
        run(slots)
    else:
        for column, picked in enumerate(cut):
            pl.when(info[total + 1] == column)(functools.partial(run, [slots[n] for n in picked]))

    if is_last:
        inside = (limits[0] >= LOWEST) & (limits[1] <= HIGHEST)

        @pl.when(jnp.max(jnp.where(inside, 0.0, 1.0)) > 0.0)
        def _():
            for n, mask in enumerate(masks(before + slots, info, total, docs, tok)):
                everything[0, n * tok:(n + 1) * tok, d:] = mask
                everything[1, n * tok:(n + 1) * tok, d:] = one

            def again(g, carry):
                for n, (_, array) in enumerate(before + slots):
                    copy = pltpu.make_async_copy(kv_refs[array].at[:, :, span(g, d)],
                                                 everything.at[:, n * tok:(n + 1) * tok, :d], sems.at[0, 0])
                    copy.start()
                    copy.wait()
                for j in range(GROUP):
                    s = scores(queries(g, j * tok, tok), everything[0])
                    top = jnp.max(s, axis=1, keepdims=True)
                    p = jnp.exp2((s - top) * SCALE).astype(jnp.bfloat16)
                    o = jnp.dot(p, everything[1], preferred_element_type=jnp.float32)
                    out_buf[0, 0, :, j * d:(j + 1) * d] = (o[:, :d] / o[:, d:]).astype(jnp.bfloat16)
                store = pltpu.make_async_copy(out_buf.at[0, 0], out_ref.at[:, span(g, wide)], sems.at[0, 0])
                store.start()
                store.wait()
                return carry

            lax.fori_loop(0, KV_HEADS, again, 0)


def attend(form, q, state, arrays, info, outs):
    total, before, slots, cut, docs, tok, rows, count, has_state, is_last = form
    d = HEAD_DIM
    n = max(len(picked) for picked in cut) if cut else len(slots)
    anywhere, here = pl.BlockSpec(memory_space=pl.ANY), pl.BlockSpec(memory_space=pltpu.VMEM)
    scratch = [pltpu.VMEM((n * tok, d), jnp.bfloat16)]
    if is_last:
        scratch += [
            pltpu.VMEM((2, UNIT, tok, GROUP * d), jnp.bfloat16),
            pltpu.VMEM((2, tok, d), jnp.float32),
            pltpu.VMEM((2, total * tok, 2 * d), jnp.bfloat16),
            pltpu.SemaphoreType.DMA((2, UNIT)),
        ]
    mine = {array for _, array in slots}
    return pl.pallas_call(
        functools.partial(kernel, form),
        out_shape=outs,
        in_specs=[pl.BlockSpec(memory_space=pltpu.SMEM)] + [here] * (1 + len(state))
        + [here if i in mine else anywhere for i in range(len(arrays))],
        out_specs=[anywhere if is_last else here] * len(outs),
        scratch_shapes=scratch,
        compiler_params=pltpu.CompilerParams(vmem_limit_bytes=(16 if total <= 16 else 60) * 1024 * 1024),
        cost_estimate=pl.CostEstimate(flops=COST * q.size, bytes_accessed=q.size, transcendentals=0),
    )(info, q, *state, *arrays)


def join(key, value):
    first = lax.broadcasted_iota(jnp.int32, (2, 1, 1), 0) == 0
    return jnp.where(first, key, value)


class Route:
    def __init__(self, devices):
        self.plane = math.isqrt(devices)
        self.cols = self.plane // 2
        self.levels = devices // self.plane
        self.reach = devices // 2 // self.plane

    def at(self, z, x, c):
        return z * self.plane + x * 2 + c

    def everyone(self, level, cores=(0, 1)):
        return [(z, x, c) for z in range(level, self.levels) for x in range(self.cols) for c in cores]

    def wanted(self, level, src, dst):
        return src < dst if level == 0 else src > dst if level == self.reach else True

    def up(self, level):
        return [(self.at(z - 1, x, c), self.at(z, x, c)) for z, x, c in self.everyone(level)]

    def across(self, level, dx, cores=(0, 1)):
        return [(self.at(z, (x - dx) % self.cols, c), self.at(z, x, c)) for z, x, c in self.everyone(level, cores)
                if self.wanted(level, (x - dx) % self.cols, x)]

    def climb(self, dx, cores):
        return [(self.at(z - 1, x, c), self.at(z, x, c)) for z, x, c in self.everyone(self.reach, cores)
                if self.wanted(self.reach, (x - dx) % self.cols, x)]

    def over(self, level, dx, cores=(0, 1)):
        return [(self.at(z, x, 1 - c), self.at(z, x, c)) for z, x, c in self.everyone(level, cores)
                if (self.wanted(level, 1 - c, c) if dx == 0 else self.wanted(level, (x - dx) % self.cols, x))]

    def carry(self, block, core, attend_early, attend_middle):
        send = lambda array, pairs: lax.ppermute(array, "head", pairs)
        reach, columns = self.reach, range(1, self.cols)
        got = {(0, 0, 0): block}

        def swap(level, dx):
            got[level, dx, 1] = send(got[level, dx, 0], self.over(level, dx))

        def tie(names, *more):
            arrays, more = lax.optimization_barrier(([got[name] for name in names], more))
            got.update(zip(names, arrays))
            return more

        state = None
        for level in range(reach):
            got[level + 1, 0, 0] = send(got[level, 0, 0], self.up(level + 1))
            for dx in columns:
                got[level, dx, 0] = send(got[level, 0, 0], self.across(level, dx))
            if level == 0:
                swap(0, 0)
            if level == 1:
                swap(1, 0)
                tie([(0, dx, 0) for dx in columns] + [(0, 0, 1)])
                state = attend_early(got)
                state, = tie([(0, dx, 0) for dx in columns] + [(1, dx, 0) for dx in columns] + [(2, 0, 0)], state)
            elif level:
                tie([(level, dx, 0) for dx in columns] + [(level + 1, 0, 0)])
        for dx in columns:
            pairs = self.across(reach, dx, (0,)) + self.climb(dx, (1,))
            got[reach, dx, 0] = send(jnp.where(core == 0, got[reach, 0, 0], got[reach - 1, dx, 0]), pairs)
        for level in range(2, reach + 1):
            swap(level, 0)
        for dx in columns:
            for level in range(reach):
                swap(level, dx)
        state, = tie([(reach, dx, 0) for dx in columns], attend_middle(got, state))
        for dx in columns:
            swap(reach, dx)
        return got, state

    def order(self):
        names = [(level, dx, other) for dx in range(self.cols) for level in range(self.reach + 1) for other in range(2)]
        early = [n for n in names if n[0] == 0 and 0 in n[1:] or n == (1, 0, 0)]
        last = [n for n in names if n[1] > 0 and (n[0] == self.reach or n[2] == 1) or n[0] > 1 and n[2] == 1]
        return early, [n for n in names if n not in early + last], last

    def block(self, name, me):
        level, dx, other = name
        z, x, c = me // self.plane, me % self.plane // 2, me % 2
        col = (x - dx + self.cols) % self.cols
        core = 1 - c if other else c
        want = self.wanted(level, core, c) if dx == 0 else self.wanted(level, col, x)
        held = (z >= level) & (want | (dx == 0 and other == 0))
        return jnp.where(held, self.at(z - level, col, core), -1)


def local(query, key, value, lengths):
    tok = query.shape[1]
    docs = lengths.shape[1]
    d = HEAD_DIM
    me = lax.axis_index("head")
    route = Route(lax.axis_size("head"))
    parts = route.order()
    names = sum(parts, [])
    total = len(names)
    base = [jnp.where(b >= 0, b * tok, FAR) for b in (route.block(name, me) for name in names)]
    info = jnp.stack(base + [me * tok, me % route.plane // 2])
    info = jnp.concatenate([info, lengths[0]]).astype(jnp.int32)
    q = query[0]
    rows = 512 if total <= 16 else 128

    def forms(part):
        if route.cols != 2 or all(name[1] == 0 or 0 < name[0] < route.reach for name in part):
            return None
        lacking = (0, route.reach)
        return [[n for n, name in enumerate(part) if name[1] == 0 or name[0] != lacking[x]] for x in range(2)]

    def work(got, stage, state):
        first = sum(len(part) for part in parts[:stage])
        is_last = stage + 1 == len(parts)
        known = names if is_last else parts[stage]
        slots = [(first + n, n + (first if is_last else 0)) for n in range(len(parts[stage]))]
        before = [(n, n) for n in range(first)]
        outs = [jax.ShapeDtypeStruct(q.shape, jnp.float32), jax.ShapeDtypeStruct((KV_HEADS, tok, d), jnp.float32)]
        if is_last:
            outs = [jax.ShapeDtypeStruct(q.shape, jnp.bfloat16)]
        form = (total, before, slots, forms(parts[stage]), docs, tok, rows, len(known), bool(state), is_last)
        return attend(form, q, state, [got[name] for name in known], info, outs)

    got, state = route.carry(join(key, value), me % 2, lambda got: work(got, 0, []), lambda got, state: work(got, 1, state))
    out, = work(got, 2, state)
    return out[None]


def solution(mesh):
    placed = (
        P("rep", "head", None),
        P("rep", "head", None),
        P("rep", "head", None),
        P("rep", None),
    )
    return jax.shard_map(
        local, mesh=mesh, in_specs=placed, out_specs=P("rep", "head", None), check_vma=False
    )
```

```python
import functools
import math

import jax
import jax.numpy as jnp
from jax import lax
from jax.experimental import pallas as pl
from jax.experimental.pallas import tpu as pltpu
from jax.sharding import PartitionSpec as P

Q_HEADS = 64
KV_HEADS = 8
HEAD_DIM = 128
GROUP = Q_HEADS // KV_HEADS
BIG = -1e30
FAR = 1 << 29
SCALE = float(HEAD_DIM) ** -0.5 * math.log2(math.e)
UNIT = 4
TILE = 256
LOWEST, HIGHEST = 2.0 ** -40, 2.0 ** 100
COST = 16


def masks(slots, info, total, docs, tok):
    q_pos = info[total] + lax.broadcasted_iota(jnp.int32, (tok, tok), 1)
    start = jnp.zeros((tok, tok), jnp.int32)
    end = jnp.int32(0)
    for doc in range(docs):
        length = info[total + 2 + doc]
        end = end + length
        start = start + jnp.where(q_pos >= end, length, 0)
    row = lax.broadcasted_iota(jnp.int32, (tok, tok), 0)
    for at, _ in slots:
        k_pos = info[at] + row
        yield jnp.where((k_pos <= q_pos) & (k_pos >= start), 0.0, BIG).astype(jnp.bfloat16)


def scores(q, k):
    return lax.dot_general(q, k, (((1,), (1,)), ((), ())), preferred_element_type=jnp.float32)


def kernel(form, info, *refs):
    total, before, slots, cut, docs, tok, rows, count, has_state, is_last = form
    d = HEAD_DIM
    wide = GROUP * d
    refs = list(refs)
    q_ref = refs.pop(0)
    state = [refs.pop(0), refs.pop(0)] if has_state else []
    kv_refs, refs = refs[:count], refs[count:]
    if is_last:
        out_ref, mask_ref, out_buf, limits, everything, sems = refs
    else:
        acc_ref, sum_ref, mask_ref = refs
    row = lax.broadcasted_iota(jnp.int32, (tok, tok), 0)
    eye = (row == lax.broadcasted_iota(jnp.int32, (tok, tok), 1)).astype(jnp.float32).astype(jnp.bfloat16)
    one = jnp.ones((tok, d), jnp.bfloat16)

    def span(g, width):
        return pl.ds(pl.multiple_of(g * width, width), width)

    def queries(g, first, rows):
        return jnp.concatenate([jnp.concatenate([q_ref[:, span(g * GROUP + j, d)], eye], axis=1)
                                for j in range(first // tok, (first + rows) // tok)], axis=0)

    def result(u, buf, h):
        return pltpu.make_async_copy(out_buf.at[buf, h], out_ref.at[:, span(u * UNIT + h, wide)], sems.at[buf, h])

    def attend(part, u, buf):
        keys = len(part) * tok
        lane = lax.broadcasted_iota(jnp.int32, (tok, d), 1)
        packed = [jnp.zeros((tok, d), jnp.float32) for _ in range(UNIT)]
        least = most = jnp.ones((tok, d), jnp.float32)
        pieces = [(h, first) for h in range(UNIT) for first in range(0, GROUP * tok, rows)]
        step = TILE // tok
        tiles = [range(low, min(low + step, len(part))) for low in range(0, len(part), step)]

        def score(piece, tile):
            g = u * UNIT + piece[0]
            k = [jnp.concatenate([kv_refs[part[n][1]][0, :, span(g, d)], mask_ref[n * tok:(n + 1) * tok, :]], axis=1)
                 for n in tile]
            return scores(queries(g, piece[1], rows), jnp.concatenate(k, axis=0))

        ahead = [score(pieces[0], tile) for tile in tiles]
        for i, (h, first) in enumerate(pieces):
            g = u * UNIT + h
            s, ahead, p = ahead, [], []
            for n, tile in enumerate(tiles):
                p.append(jnp.exp2(s[n] * SCALE).astype(jnp.bfloat16))
                if i + 1 < len(pieces):
                    ahead.append(score(pieces[i + 1], tile))
            v = [jnp.concatenate([kv_refs[array][1, :, span(g, d)], one], axis=1) for _, array in part]
            o = jnp.dot(jnp.concatenate(p, axis=1), jnp.concatenate(v, axis=0), preferred_element_type=jnp.float32)
            heads = range(first // tok, (first + rows) // tok)
            accs = [o[n * tok:(n + 1) * tok, :d] for n in range(len(heads))]
            if has_state:
                accs = [acc + state[0][:, span(g * GROUP + j, d)] for acc, j in zip(accs, heads)]
            for n, j in enumerate(heads):
                packed[h] = jnp.where(lane == j, o[n * tok:(n + 1) * tok, d:], packed[h])
            if is_last:
                row_sum = packed[h] + state[1][g]
                row_sum = jnp.where((lane >= heads[0]) & (lane <= heads[-1]), row_sum, 1.0)
                least, most = jnp.minimum(least, row_sum), jnp.maximum(most, row_sum)
                share = pl.reciprocal(row_sum, approx=True)
                share = share * (2.0 - row_sum * share)
            for acc, j in zip(accs, heads):
                if is_last:
                    out_buf[buf, h, :, j * d:(j + 1) * d] = (acc * share[:, j:j + 1]).astype(jnp.bfloat16)
                else:
                    acc_ref[:, span(g * GROUP + j, d)] = acc
            if is_last and first + rows == GROUP * tok:
                result(u, buf, h).start()
        if is_last:
            limits[0] = jnp.minimum(limits[0], least)
            limits[1] = jnp.maximum(limits[1], most)
        else:
            for h in range(UNIT):
                sum_ref[u * UNIT + h] = packed[h] + state[1][u * UNIT + h] if has_state else packed[h]

    def run(part):
        units = KV_HEADS // UNIT
        for n, mask in enumerate(masks(part, info, total, docs, tok)):
            mask_ref[n * tok:(n + 1) * tok, :] = mask
        if is_last:
            limits[...] = jnp.ones((2, tok, d), jnp.float32)

        def step(u, carry):
            buf = lax.rem(u, 2)
            if is_last:
                @pl.when(u > 1)
                def _():
                    for h in range(UNIT):
                        result(u - 2, buf, h).wait()
            attend(part, u, buf)
            return carry

        lax.fori_loop(0, units, step, 0)
        if is_last:
            for u in range(units - 2, units):
                for h in range(UNIT):
                    result(u, u % 2, h).wait()

    if cut is None:
        run(slots)
    else:
        for column, picked in enumerate(cut):
            pl.when(info[total + 1] == column)(functools.partial(run, [slots[n] for n in picked]))

    if is_last:
        inside = (limits[0] >= LOWEST) & (limits[1] <= HIGHEST)

        @pl.when(jnp.max(jnp.where(inside, 0.0, 1.0)) > 0.0)
        def _():
            for n, mask in enumerate(masks(before + slots, info, total, docs, tok)):
                everything[0, n * tok:(n + 1) * tok, d:] = mask
                everything[1, n * tok:(n + 1) * tok, d:] = one

            def again(g, carry):
                for n, (_, array) in enumerate(before + slots):
                    copy = pltpu.make_async_copy(kv_refs[array].at[:, :, span(g, d)],
                                                 everything.at[:, n * tok:(n + 1) * tok, :d], sems.at[0, 0])
                    copy.start()
                    copy.wait()
                for j in range(GROUP):
                    s = scores(queries(g, j * tok, tok), everything[0])
                    top = jnp.max(s, axis=1, keepdims=True)
                    p = jnp.exp2((s - top) * SCALE).astype(jnp.bfloat16)
                    o = jnp.dot(p, everything[1], preferred_element_type=jnp.float32)
                    out_buf[0, 0, :, j * d:(j + 1) * d] = (o[:, :d] / o[:, d:]).astype(jnp.bfloat16)
                store = pltpu.make_async_copy(out_buf.at[0, 0], out_ref.at[:, span(g, wide)], sems.at[0, 0])
                store.start()
                store.wait()
                return carry

            lax.fori_loop(0, KV_HEADS, again, 0)


def attend(form, q, state, arrays, info, outs):
    total, before, slots, cut, docs, tok, rows, count, has_state, is_last = form
    d = HEAD_DIM
    n = max(len(picked) for picked in cut) if cut else len(slots)
    anywhere, here = pl.BlockSpec(memory_space=pl.ANY), pl.BlockSpec(memory_space=pltpu.VMEM)
    scratch = [pltpu.VMEM((n * tok, d), jnp.bfloat16)]
    if is_last:
        scratch += [
            pltpu.VMEM((2, UNIT, tok, GROUP * d), jnp.bfloat16),
            pltpu.VMEM((2, tok, d), jnp.float32),
            pltpu.VMEM((2, total * tok, 2 * d), jnp.bfloat16),
            pltpu.SemaphoreType.DMA((2, UNIT)),
        ]
    mine = {array for _, array in slots}
    return pl.pallas_call(
        functools.partial(kernel, form),
        out_shape=outs,
        in_specs=[pl.BlockSpec(memory_space=pltpu.SMEM)] + [here] * (1 + len(state))
        + [here if i in mine else anywhere for i in range(len(arrays))],
        out_specs=[anywhere if is_last else here] * len(outs),
        scratch_shapes=scratch,
        compiler_params=pltpu.CompilerParams(vmem_limit_bytes=(16 if total <= 16 else 60) * 1024 * 1024),
        cost_estimate=pl.CostEstimate(flops=COST * q.size, bytes_accessed=q.size, transcendentals=0),
    )(info, q, *state, *arrays)


def join(key, value):
    first = lax.broadcasted_iota(jnp.int32, (2, 1, 1), 0) == 0
    return jnp.where(first, key, value)


class Route:
    def __init__(self, devices):
        self.plane = math.isqrt(devices)
        self.cols = self.plane // 2
        self.levels = devices // self.plane
        self.reach = devices // 2 // self.plane

    def at(self, z, x, c):
        return z * self.plane + x * 2 + c

    def everyone(self, level, cores=(0, 1)):
        return [(z, x, c) for z in range(level, self.levels) for x in range(self.cols) for c in cores]

    def wanted(self, level, src, dst):
        return src < dst if level == 0 else src > dst if level == self.reach else True

    def up(self, level):
        return [(self.at(z - 1, x, c), self.at(z, x, c)) for z, x, c in self.everyone(level)]

    def across(self, level, dx, cores=(0, 1)):
        return [(self.at(z, (x - dx) % self.cols, c), self.at(z, x, c)) for z, x, c in self.everyone(level, cores)
                if self.wanted(level, (x - dx) % self.cols, x)]

    def climb(self, dx, cores):
        return [(self.at(z - 1, x, c), self.at(z, x, c)) for z, x, c in self.everyone(self.reach, cores)
                if self.wanted(self.reach, (x - dx) % self.cols, x)]

    def over(self, level, dx, cores=(0, 1)):
        return [(self.at(z, x, 1 - c), self.at(z, x, c)) for z, x, c in self.everyone(level, cores)
                if (self.wanted(level, 1 - c, c) if dx == 0 else self.wanted(level, (x - dx) % self.cols, x))]

    def carry(self, block, core, attend_early, attend_middle):
        send = lambda array, pairs: lax.ppermute(array, "head", pairs)
        reach, columns = self.reach, range(1, self.cols)
        got = {(0, 0, 0): block}

        def swap(level, dx):
            got[level, dx, 1] = send(got[level, dx, 0], self.over(level, dx))

        def tie(names, *more):
            arrays, more = lax.optimization_barrier(([got[name] for name in names], more))
            got.update(zip(names, arrays))
            return more

        state = None
        for level in range(reach):
            got[level + 1, 0, 0] = send(got[level, 0, 0], self.up(level + 1))
            for dx in columns:
                got[level, dx, 0] = send(got[level, 0, 0], self.across(level, dx))
            if level == 0:
                swap(0, 0)
            if level == 1:
                swap(1, 0)
                tie([(0, dx, 0) for dx in columns] + [(0, 0, 1)])
                state = attend_early(got)
                state, = tie([(0, dx, 0) for dx in columns] + [(1, dx, 0) for dx in columns] + [(2, 0, 0)], state)
            elif level:
                tie([(level, dx, 0) for dx in columns] + [(level + 1, 0, 0)])
        for dx in columns:
            pairs = self.across(reach, dx, (0,)) + self.climb(dx, (1,))
            got[reach, dx, 0] = send(jnp.where(core == 0, got[reach, 0, 0], got[reach - 1, dx, 0]), pairs)
        for dx in columns:
            for level in reversed(range(reach)):
                swap(level, dx)
        for level in range(2, reach + 1):
            swap(level, 0)
        state, = tie([(reach, dx, 0) for dx in columns], attend_middle(got, state))
        for dx in columns:
            swap(reach, dx)
        return got, state

    def order(self):
        names = [(level, dx, other) for dx in range(self.cols) for level in range(self.reach + 1) for other in range(2)]
        early = [n for n in names if n[0] == 0 and 0 in n[1:] or n == (1, 0, 0)]
        last = [n for n in names if n[1] > 0 and (n[0] == self.reach or n[2] == 1) or n[0] > 1 and n[2] == 1]
        return early, [n for n in names if n not in early + last], last

    def block(self, name, me):
        level, dx, other = name
        z, x, c = me // self.plane, me % self.plane // 2, me % 2
        col = (x - dx + self.cols) % self.cols
        core = 1 - c if other else c
        want = self.wanted(level, core, c) if dx == 0 else self.wanted(level, col, x)
        held = (z >= level) & (want | (dx == 0 and other == 0))
        return jnp.where(held, self.at(z - level, col, core), -1)


def local(query, key, value, lengths):
    tok = query.shape[1]
    docs = lengths.shape[1]
    d = HEAD_DIM
    me = lax.axis_index("head")
    route = Route(lax.axis_size("head"))
    parts = route.order()
    names = sum(parts, [])
    total = len(names)
    base = [jnp.where(b >= 0, b * tok, FAR) for b in (route.block(name, me) for name in names)]
    info = jnp.stack(base + [me * tok, me % route.plane // 2])
    info = jnp.concatenate([info, lengths[0]]).astype(jnp.int32)
    q = query[0]
    rows = 512 if total <= 16 else 128

    def forms(part):
        if route.cols != 2 or all(name[1] == 0 or 0 < name[0] < route.reach for name in part):
            return None
        lacking = (0, route.reach)
        return [[n for n, name in enumerate(part) if name[1] == 0 or name[0] != lacking[x]] for x in range(2)]

    def work(got, stage, state):
        first = sum(len(part) for part in parts[:stage])
        is_last = stage + 1 == len(parts)
        known = names if is_last else parts[stage]
        slots = [(first + n, n + (first if is_last else 0)) for n in range(len(parts[stage]))]
        before = [(n, n) for n in range(first)]
        outs = [jax.ShapeDtypeStruct(q.shape, jnp.float32), jax.ShapeDtypeStruct((KV_HEADS, tok, d), jnp.float32)]
        if is_last:
            outs = [jax.ShapeDtypeStruct(q.shape, jnp.bfloat16)]
        form = (total, before, slots, forms(parts[stage]), docs, tok, rows, len(known), bool(state), is_last)
        return attend(form, q, state, [got[name] for name in known], info, outs)

    got, state = route.carry(join(key, value), me % 2, lambda got: work(got, 0, []), lambda got, state: work(got, 1, state))
    out, = work(got, 2, state)
    return out[None]


def solution(mesh):
    placed = (
        P("rep", "head", None),
        P("rep", "head", None),
        P("rep", "head", None),
        P("rep", None),
    )
    return jax.shard_map(
        local, mesh=mesh, in_specs=placed, out_specs=P("rep", "head", None), check_vma=False
    )
```

```python
import functools
import itertools
import math

import jax
import jax.numpy as jnp
from jax import lax
from jax.experimental import pallas as pl
from jax.experimental.pallas import tpu as pltpu
from jax.sharding import PartitionSpec as P

Q_HEADS = 64
KV_HEADS = 8
HEAD_DIM = 128
GROUP = Q_HEADS // KV_HEADS
BIG = -1e30
FAR = 1 << 29
SCALE = float(HEAD_DIM) ** -0.5 * math.log2(math.e)
UNIT = 4
TILE = 256
LOWEST, HIGHEST = 2.0 ** -40, 2.0 ** 100
COST = 16


def masks(slots, info, total, docs, tok):
    q_pos = info[total] + lax.broadcasted_iota(jnp.int32, (tok, tok), 1)
    start = jnp.zeros((tok, tok), jnp.int32)
    end = jnp.int32(0)
    for doc in range(docs):
        length = info[total + 2 + doc]
        end = end + length
        start = start + jnp.where(q_pos >= end, length, 0)
    row = lax.broadcasted_iota(jnp.int32, (tok, tok), 0)
    for at, _ in slots:
        k_pos = info[at] + row
        yield jnp.where((k_pos <= q_pos) & (k_pos >= start), 0.0, BIG).astype(jnp.bfloat16)


def scores(q, k):
    return lax.dot_general(q, k, (((1,), (1,)), ((), ())), preferred_element_type=jnp.float32)


def kernel(form, info, *refs):
    total, before, slots, cut, docs, tok, rows, count, has_state, is_last = form
    d = HEAD_DIM
    wide = GROUP * d
    refs = list(refs)
    q_ref = refs.pop(0)
    state = [refs.pop(0), refs.pop(0)] if has_state else []
    kv_refs, refs = refs[:count], refs[count:]
    if is_last:
        out_ref, mask_ref, out_buf, limits, everything, sems = refs
    else:
        acc_ref, sum_ref, mask_ref = refs
    row = lax.broadcasted_iota(jnp.int32, (tok, tok), 0)
    eye = (row == lax.broadcasted_iota(jnp.int32, (tok, tok), 1)).astype(jnp.float32).astype(jnp.bfloat16)
    one = jnp.ones((tok, d), jnp.bfloat16)

    def span(g, width):
        return pl.ds(pl.multiple_of(g * width, width), width)

    def queries(g, first, rows):
        return jnp.concatenate([jnp.concatenate([q_ref[:, span(g * GROUP + j, d)], eye], axis=1)
                                for j in range(first // tok, (first + rows) // tok)], axis=0)

    def results(u, buf, h):
        share = rows * d // tok
        for n in range(wide // share):
            yield pltpu.make_async_copy(out_buf.at[buf, h, :, n * share:(n + 1) * share],
                                        out_ref.at[:, span((u * UNIT + h) * (wide // share) + n, share)],
                                        sems.at[buf, h, n])

    def attend(part, u, buf):
        keys = len(part) * tok
        lane = lax.broadcasted_iota(jnp.int32, (tok, d), 1)
        packed = [jnp.zeros((tok, d), jnp.float32) for _ in range(UNIT)]
        least = most = jnp.ones((tok, d), jnp.float32)
        pieces = [(h, first) for h in range(UNIT) for first in range(0, GROUP * tok, rows)]
        step = TILE // tok
        tiles = [range(low, min(low + step, len(part))) for low in range(0, len(part), step)]

        def score(piece, tile):
            g = u * UNIT + piece[0]
            k = [jnp.concatenate([kv_refs[part[n][1]][0, :, span(g, d)], mask_ref[n * tok:(n + 1) * tok, :]], axis=1)
                 for n in tile]
            return scores(queries(g, piece[1], rows), jnp.concatenate(k, axis=0))

        ahead = [score(pieces[0], tile) for tile in tiles]
        for i, (h, first) in enumerate(pieces):
            g = u * UNIT + h
            s, ahead, p = ahead, [], []
            for n, tile in enumerate(tiles):
                p.append(jnp.exp2(s[n] * SCALE).astype(jnp.bfloat16))
                if i + 1 < len(pieces):
                    ahead.append(score(pieces[i + 1], tile))
            v = [jnp.concatenate([kv_refs[array][1, :, span(g, d)], one], axis=1) for _, array in part]
            o = jnp.dot(jnp.concatenate(p, axis=1), jnp.concatenate(v, axis=0), preferred_element_type=jnp.float32)
            for n in range(rows // tok):
                j = first // tok + n
                acc, row_sum = o[n * tok:(n + 1) * tok, :d], o[n * tok:(n + 1) * tok, d:]
                if has_state:
                    acc = acc + state[0][:, span(g * GROUP + j, d)]
                if is_last:
                    row_sum = row_sum + state[1][g, :, j:j + 1]
                    least, most = jnp.minimum(least, row_sum), jnp.maximum(most, row_sum)
                    share = pl.reciprocal(row_sum, approx=True)
                    share = share * (2.0 - row_sum * share)
                    out_buf[buf, h, :, j * d:(j + 1) * d] = (acc * share).astype(jnp.bfloat16)
                else:
                    packed[h] = jnp.where(lane == j, row_sum, packed[h])
                    acc_ref[:, span(g * GROUP + j, d)] = acc
            if is_last:
                next(itertools.islice(results(u, buf, h), first // rows, None)).start()
        if is_last:
            limits[0] = jnp.minimum(limits[0], least)
            limits[1] = jnp.maximum(limits[1], most)
        else:
            for h in range(UNIT):
                sum_ref[u * UNIT + h] = packed[h] + state[1][u * UNIT + h] if has_state else packed[h]

    def run(part):
        units = KV_HEADS // UNIT
        for n, mask in enumerate(masks(part, info, total, docs, tok)):
            mask_ref[n * tok:(n + 1) * tok, :] = mask
        if is_last:
            limits[...] = jnp.ones((2, tok, d), jnp.float32)

        def step(u, carry):
            buf = lax.rem(u, 2)
            if is_last:
                @pl.when(u > 1)
                def _():
                    for h in range(UNIT):
                        for copy in results(u - 2, buf, h):
                            copy.wait()
            attend(part, u, buf)
            return carry

        lax.fori_loop(0, units, step, 0)

    if cut is None:
        run(slots)
    else:
        for column, picked in enumerate(cut):
            pl.when(info[total + 1] == column)(functools.partial(run, [slots[n] for n in picked]))

    if is_last:
        inside = (limits[0] >= LOWEST) & (limits[1] <= HIGHEST)
        beyond = jnp.max(jnp.where(inside, 0.0, 1.0)) > 0.0
        for u in range(KV_HEADS // UNIT - 2, KV_HEADS // UNIT):
            for h in range(UNIT):
                for copy in results(u, u % 2, h):
                    copy.wait()

        @pl.when(beyond)
        def _():
            for n, mask in enumerate(masks(before + slots, info, total, docs, tok)):
                everything[0, n * tok:(n + 1) * tok, d:] = mask
                everything[1, n * tok:(n + 1) * tok, d:] = one

            def again(g, carry):
                for n, (_, array) in enumerate(before + slots):
                    copy = pltpu.make_async_copy(kv_refs[array].at[:, :, span(g, d)],
                                                 everything.at[:, n * tok:(n + 1) * tok, :d], sems.at[0, 0, 0])
                    copy.start()
                    copy.wait()
                for j in range(GROUP):
                    s = scores(queries(g, j * tok, tok), everything[0])
                    top = jnp.max(s, axis=1, keepdims=True)
                    p = jnp.exp2((s - top) * SCALE).astype(jnp.bfloat16)
                    o = jnp.dot(p, everything[1], preferred_element_type=jnp.float32)
                    out_buf[0, 0, :, j * d:(j + 1) * d] = (o[:, :d] / o[:, d:]).astype(jnp.bfloat16)
                store = pltpu.make_async_copy(out_buf.at[0, 0], out_ref.at[:, span(g, wide)], sems.at[0, 0, 0])
                store.start()
                store.wait()
                return carry

            lax.fori_loop(0, KV_HEADS, again, 0)


def attend(form, q, state, arrays, info, outs):
    total, before, slots, cut, docs, tok, rows, count, has_state, is_last = form
    d = HEAD_DIM
    n = max(len(picked) for picked in cut) if cut else len(slots)
    anywhere, here = pl.BlockSpec(memory_space=pl.ANY), pl.BlockSpec(memory_space=pltpu.VMEM)
    scratch = [pltpu.VMEM((n * tok, d), jnp.bfloat16)]
    if is_last:
        scratch += [
            pltpu.VMEM((2, UNIT, tok, GROUP * d), jnp.bfloat16),
            pltpu.VMEM((2, tok, d), jnp.float32),
            pltpu.VMEM((2, total * tok, 2 * d), jnp.bfloat16),
            pltpu.SemaphoreType.DMA((2, UNIT, GROUP * tok // rows)),
        ]
    mine = {array for _, array in slots}
    return pl.pallas_call(
        functools.partial(kernel, form),
        out_shape=outs,
        in_specs=[pl.BlockSpec(memory_space=pltpu.SMEM)] + [here] * (1 + len(state))
        + [here if i in mine else anywhere for i in range(len(arrays))],
        out_specs=[anywhere if is_last else here] * len(outs),
        scratch_shapes=scratch,
        compiler_params=pltpu.CompilerParams(vmem_limit_bytes=(24 if total <= 16 else 60) * 1024 * 1024),
        cost_estimate=pl.CostEstimate(flops=COST * q.size, bytes_accessed=q.size, transcendentals=0),
    )(info, q, *state, *arrays)


def join(key, value):
    first = lax.broadcasted_iota(jnp.int32, (2, 1, 1), 0) == 0
    return jnp.where(first, key, value)


class Route:
    def __init__(self, devices):
        self.plane = math.isqrt(devices)
        self.cols = self.plane // 2
        self.levels = devices // self.plane
        self.reach = devices // 2 // self.plane

    def at(self, z, x, c):
        return z * self.plane + x * 2 + c

    def everyone(self, level, cores=(0, 1)):
        return [(z, x, c) for z in range(level, self.levels) for x in range(self.cols) for c in cores]

    def wanted(self, level, src, dst):
        return src < dst if level == 0 else src > dst if level == self.reach else True

    def up(self, level):
        return [(self.at(z - 1, x, c), self.at(z, x, c)) for z, x, c in self.everyone(level)]

    def across(self, level, dx, cores=(0, 1)):
        return [(self.at(z, (x - dx) % self.cols, c), self.at(z, x, c)) for z, x, c in self.everyone(level, cores)
                if self.wanted(level, (x - dx) % self.cols, x)]

    def climb(self, dx, cores):
        return [(self.at(z - 1, x, c), self.at(z, x, c)) for z, x, c in self.everyone(self.reach, cores)
                if self.wanted(self.reach, (x - dx) % self.cols, x)]

    def over(self, level, dx, cores=(0, 1)):
        return [(self.at(z, x, 1 - c), self.at(z, x, c)) for z, x, c in self.everyone(level, cores)
                if (level or c if dx == 0 else self.wanted(level, (x - dx) % self.cols, x))]

    def carry(self, block, core, attend_early, attend_middle):
        send = lambda array, pairs: lax.ppermute(array, "head", pairs)
        reach, columns = self.reach, range(1, self.cols)
        got = {(0, 0, 0): block}

        def swap(level, dx):
            got[level, dx, 1] = send(got[level, dx, 0], self.over(level, dx))

        def tie(names, *more):
            arrays, more = lax.optimization_barrier(([got[name] for name in names], more))
            got.update(zip(names, arrays))
            return more

        state = None
        for level in range(reach):
            got[level + 1, 0, 0] = send(got[level, 0, 0], self.up(level + 1))
            for dx in columns:
                got[level, dx, 0] = send(got[level, 0, 0], self.across(level, dx))
            if level == 0:
                swap(0, 0)
            if level == 1:
                swap(1, 0)
                tie([(0, dx, 0) for dx in columns] + [(0, 0, 1)])
                state = attend_early(got)
                state, = tie([(0, dx, 0) for dx in columns] + [(1, dx, 0) for dx in columns] + [(2, 0, 0)], state)
            elif level:
                tie([(level, dx, 0) for dx in columns] + [(level + 1, 0, 0)])
        for dx in columns:
            pairs = self.across(reach, dx, (0,)) + self.climb(dx, (1,))
            got[reach, dx, 0] = send(jnp.where(core == 0, got[reach, 0, 0], got[reach - 1, dx, 0]), pairs)
        for level in range(2, reach + 1):
            swap(level, 0)
        for dx in columns:
            for level in range(reach):
                swap(level, dx)
        state, = tie([(reach, dx, 0) for dx in columns], attend_middle(got, state))
        for dx in columns:
            swap(reach, dx)
        return got, state

    def order(self):
        names = [(level, dx, other) for dx in range(self.cols) for level in range(self.reach + 1) for other in range(2)]
        early = [n for n in names if n[0] == 0 and 0 in n[1:] or n == (1, 0, 0)]
        last = [n for n in names if n[1] > 0 and (n[0] == self.reach or n[2] == 1) or n[0] > 1 and n[2] == 1]
        return early, [n for n in names if n not in early + last], last

    def block(self, name, me):
        level, dx, other = name
        z, x, c = me // self.plane, me % self.plane // 2, me % 2
        col = (x - dx + self.cols) % self.cols
        core = 1 - c if other else c
        want = self.wanted(level, core, c) if dx == 0 else self.wanted(level, col, x)
        held = (z >= level) & (want | (dx == 0 and other == 0))
        return jnp.where(held, self.at(z - level, col, core), -1)


def local(query, key, value, lengths):
    tok = query.shape[1]
    docs = lengths.shape[1]
    d = HEAD_DIM
    me = lax.axis_index("head")
    route = Route(lax.axis_size("head"))
    parts = route.order()
    names = sum(parts, [])
    total = len(names)
    base = [jnp.where(b >= 0, b * tok, FAR) for b in (route.block(name, me) for name in names)]
    info = jnp.stack(base + [me * tok, me % route.plane // 2])
    info = jnp.concatenate([info, lengths[0]]).astype(jnp.int32)
    q = query[0]
    rows = 1024 if total <= 16 else 128

    def forms(part):
        if route.cols != 2 or all(name[1] == 0 or 0 < name[0] < route.reach for name in part):
            return None
        lacking = (0, route.reach)
        return [[n for n, name in enumerate(part) if name[1] == 0 or name[0] != lacking[x]] for x in range(2)]

    def work(got, stage, state):
        first = sum(len(part) for part in parts[:stage])
        is_last = stage + 1 == len(parts)
        known = names if is_last else parts[stage]
        slots = [(first + n, n + (first if is_last else 0)) for n in range(len(parts[stage]))]
        before = [(n, n) for n in range(first)]
        outs = [jax.ShapeDtypeStruct(q.shape, jnp.float32), jax.ShapeDtypeStruct((KV_HEADS, tok, d), jnp.float32)]
        if is_last:
            outs = [jax.ShapeDtypeStruct(q.shape, jnp.bfloat16)]
        form = (total, before, slots, forms(parts[stage]), docs, tok, rows, len(known), bool(state), is_last)
        return attend(form, q, state, [got[name] for name in known], info, outs)

    got, state = route.carry(join(key, value), me % 2, lambda got: work(got, 0, []), lambda got, state: work(got, 1, state))
    out, = work(got, 2, state)
    return out[None]


def solution(mesh):
    placed = (
        P("rep", "head", None),
        P("rep", "head", None),
        P("rep", "head", None),
        P("rep", None),
    )
    return jax.shard_map(
        local, mesh=mesh, in_specs=placed, out_specs=P("rep", "head", None), check_vma=False
    )
```
